32 devices in a mesh: samp: 8 (over z, y), feat: 4 (over x, core).
Axes of the slice: x: 2, y: 2, z: 4, core: 2. Of those that a mesh axis runs over, the one named last changes fastest.
Arguments:
- states: bfloat16 [8192, 16384], P('samp', 'feat'), may hold values from -0.176776695 to 0.176776695
- targets: float32 [8192, 128], P('samp'), may hold values from -40 to 40
- penalty: float32 [128], replicated, may hold values from 0.1 to 1
Outputs:
- readout: float32 [16384, 128], P('feat')
- residual: float32 [8192, 128], P('samp')
The draws below stay inside these ranges and needn't reach their ends.
All inputs are finite; a program needn't handle non-finite values.
Results may differ from the reference program's by a relative error of at most 0.0058.
Values may be sent and summed in bfloat16 or wider, within the bound.
A program may use at most 64 MiB of HBM per device.

```python
import math
import jax
import jax.numpy as jnp

F = 16384
C = 128
ITERS = 3
SAMPLES = 8192


def draw_states(key, part):
    key_base, key_cols, key_shared, key_load = jax.random.split(key, 4)
    column_scale = jnp.exp(jax.random.uniform(key_cols, (1, F), jnp.float32, math.log(0.1), math.log(3.0)))
    loading = jax.random.uniform(key_load, (1, F), jnp.float32, 0.5, 1.5)
    base = jnp.clip(jax.random.normal(key_base, (SAMPLES, F), jnp.float32), -4.0, 4.0)
    shared = jnp.clip(jax.random.normal(key_shared, (SAMPLES, 1), jnp.float32), -3.0, 3.0)
    common = 8.0 / math.sqrt(F) * shared * loading
    return ((base * column_scale + common) * (1.0 / math.sqrt(SAMPLES))).astype(jnp.bfloat16)


def draw_targets(key, part):
    key_rows, key_cols, key_base = jax.random.split(key, 3)
    row_scale = jnp.exp(jax.random.uniform(key_rows, (SAMPLES, 1), jnp.float32, math.log(0.3), math.log(3.0)))
    column_scale = jnp.exp(jax.random.uniform(key_cols, (1, C), jnp.float32, math.log(0.3), math.log(3.0)))
    base = jnp.clip(jax.random.normal(key_base, (SAMPLES, C), jnp.float32), -4.0, 4.0)
    return base * row_scale * column_scale


def setup_inputs(seed: int = 0) -> dict:
    arg_keys = jax.random.split(jax.random.key(seed), 4)
    states = draw_states(jax.random.fold_in(arg_keys[3], 71), 0)
    targets = draw_targets(jax.random.fold_in(arg_keys[3], 71), 0)
    penalty = jnp.clip(jnp.exp(jax.random.uniform(arg_keys[2], (C,), jnp.float32, math.log(0.1), math.log(1.0))), 0.1, 1.0)
    return dict(states=states, targets=targets, penalty=penalty)


def reference(states, targets, penalty):
    readout = jnp.zeros((F, C), jnp.float32)
    residual = targets
    residual_b = residual.astype(jnp.bfloat16)
    gradient = jnp.dot(states.T, residual_b, preferred_element_type=jnp.float32) - penalty * readout
    direction = gradient
    norm_now = jnp.sum(gradient * gradient, axis=0)
    for step in range(ITERS):
        direction_b = direction.astype(jnp.bfloat16)
        image = jnp.dot(states, direction_b, preferred_element_type=jnp.float32)
        curvature = jnp.sum(image * image, axis=0) + penalty * jnp.sum(direction * direction, axis=0)
        step_size = norm_now / curvature
        readout = readout + step_size * direction
        residual = residual - step_size * image
        if step + 1 < ITERS:
            residual_b = residual.astype(jnp.bfloat16)
            gradient = jnp.dot(states.T, residual_b, preferred_element_type=jnp.float32) - penalty * readout
            norm_next = jnp.sum(gradient * gradient, axis=0)
            direction = gradient + (norm_next / norm_now) * direction
            norm_now = norm_next
    return readout, residual
```

```python
import functools
import jax
import jax.numpy as jnp
from jax import lax
from jax.experimental import pallas as pl
from jax.experimental.pallas import tpu as pltpu
from jax.sharding import PartitionSpec as P

ITERS = 3
F32 = jnp.float32
BF16 = jnp.bfloat16


def flip(index, mask):
    out = index
    bit = 1
    while bit <= mask:
        if mask & bit:
            out = out + bit - 2 * bit * ((index // bit) % 2)
        bit *= 2
    return out


def to_rows(columns):
    channels = columns[0].shape[0]
    lane = lax.broadcasted_iota(jnp.int32, (channels, 128), 1)
    block = jnp.zeros((channels, 128), F32)
    for i, column in enumerate(columns):
        block = jnp.where(lane == i, column, block)
    return jnp.transpose(block)[:8]


def to_columns(rows, count):
    channels = rows.shape[1]
    block = jnp.concatenate([rows, jnp.zeros((128 - 8, channels), F32)], axis=0)
    block = jnp.transpose(block)
    return [block[:, i : i + 1] for i in range(count)]


def kernel(
    n_samp, a_hbm, t_ref, pen_ref, x_out, r_out,
    a, vb, r, acc, rs_send, rs_recv, ag, d, x, qa, q, sm, cu,
    c1_send, c1_recv, c1s_send, c1s_recv, x2_send, x2_recv, x2s_send, x2s_recv, c3_recv,
    a_sem, rs_ss, rs_rs, ag_ss, ag_rs, sm_ss, sm_rs, cu_ss, cu_rs, f_ss, f_rs,
):
    chunk = a.shape[2]
    half = a.shape[1] // 2
    me = lax.axis_index("samp")
    feat = lax.axis_index("feat")
    core = feat % 2
    peers = sorted(range(1, n_samp), key=lambda o: (-(o // 4), o))
    near = list(range(1, n_samp))
    other_core = {"feat": flip(feat, 1)}
    other_x = {"feat": flip(feat, 2)}

    def load(o, h):
        rows = pl.ds(pl.multiple_of(flip(core, h) * half, half), half)
        columns = pl.ds(pl.multiple_of(flip(me, o) * chunk, chunk), chunk)
        return pltpu.make_async_copy(
            a_hbm.at[rows, columns], a.at[o, pl.ds(h * half, half)], a_sem.at[o, h]
        )

    for o in peers + [0]:
        for h in range(2):
            load(o, h).start()

    barrier = pltpu.get_barrier_semaphore()
    for o in near:
        pl.semaphore_signal(barrier, inc=1, device_id={"samp": flip(me, o)})
    for partner in (other_core, other_x):
        pl.semaphore_signal(barrier, inc=1, device_id=partner)

    pen = pen_ref[...]
    for h in range(2):
        r[h] = t_ref[:, pl.ds(pl.multiple_of(flip(core, h) * half, half), half)]
    d[...] = jnp.zeros_like(d)
    x[...] = jnp.zeros_like(x)
    q[...] = jnp.zeros_like(q)
    pl.semaphore_wait(barrier, n_samp - 1 + 2)

    def send(src, dst, ss, rs, target):
        copy = pltpu.make_async_remote_copy(
            src_ref=src, dst_ref=dst, send_sem=ss, recv_sem=rs, device_id=target,
        )
        copy.start()
        return copy

    def row_sum(value):
        return jnp.sum(value, axis=1, keepdims=True)

    def advance(o, last, alpha, beta):
        new = ag[last, o].astype(F32) + beta * d[o]
        d[o] = new
        x[o] = x[o] + alpha * new

    def step(k, carry):
        norm, dsq, alpha, beta = carry
        for h in range(2):
            vb[:, h * half : (h + 1) * half] = r[h].astype(BF16)

        def project(o):
            @pl.when(k == 0)
            def _():
                for h in range(2):
                    load(o, h).wait()

            return jnp.dot(vb[...], a[o], preferred_element_type=F32)

        sent = {}
        for o in peers:
            rs_send[o] = project(o).astype(BF16)
            sent[o] = send(
                rs_send.at[o], rs_recv.at[k, o], rs_ss.at[o], rs_rs.at[k, o], {"samp": flip(me, o)}
            )
        acc[...] = project(0)

        @pl.when(k > 0)
        def _():
            for o in range(n_samp):
                advance(o, k - 1, alpha, beta)

        for o in near:
            sent[o].wait_recv()
            acc[...] += rs_recv[k, o].astype(F32)
        g = acc[...] - pen * x[0]
        gb = g.astype(BF16)
        ag[k, 0] = gb
        gathered, small = {}, {}
        for o in peers:
            gathered[o] = send(
                ag.at[k, 0], ag.at[k, o], ag_ss.at[o], ag_rs.at[k, o], {"samp": flip(me, o)}
            )
        gf = gb.astype(F32)
        sm[k, me] = to_rows([row_sum(g * g), row_sum(gf * gf), row_sum(gf * d[0])])
        for o in peers:
            small[o] = send(
                sm.at[k, me], sm.at[k, me], sm_ss.at[o], sm_rs.at[k, o], {"samp": flip(me, o)}
            )
        for o in near:
            sent[o].wait_send()

        def image_of(o):
            return lax.dot_general(
                ag[k, o], a[o], (((1,), (1,)), ((), ())), preferred_element_type=F32
            )

        qa[...] = image_of(0)
        for o in near:
            gathered[o].wait_recv()
            qa[...] += image_of(o)

        c1_send[...] = qa[:, half:].astype(BF16)
        c1 = send(c1_send, c1_recv.at[k], f_ss.at[0], f_rs.at[k, 0], other_core)
        for o in near:
            small[o].wait_recv()
        sums = sm[k, 0]
        for i in range(1, n_samp):
            sums = sums + sm[k, i]
        c1s_send[...] = sums
        c1s = send(c1s_send, c1s_recv.at[k], f_ss.at[1], f_rs.at[k, 1], other_core)
        c1.wait()
        x2_send[...] = (qa[:, :half] + c1_recv[k].astype(F32)).astype(BF16)
        x2 = send(x2_send, x2_recv.at[k], f_ss.at[2], f_rs.at[k, 2], other_x)
        c1s.wait()
        sums = sums + c1s_recv[k]
        x2s_send[...] = sums
        x2s = send(x2s_send, x2s_recv.at[k], f_ss.at[3], f_rs.at[k, 3], other_x)
        for o in near:
            gathered[o].wait_send()
            small[o].wait_send()
        x2s.wait()
        sums = sums + x2s_recv[k]
        norm_next, gbsq, gd = to_columns(sums, 3)
        beta = jnp.where(k == 0, 0.0, norm_next / norm)
        dsq = gbsq + 2.0 * beta * gd + beta * beta * dsq
        x2.wait()
        mine = x2_send[...].astype(F32) + x2_recv[k].astype(F32) + beta * q[...]
        q[...] = mine
        c3 = send(q, c3_recv.at[k], f_ss.at[4], f_rs.at[k, 4], other_core)
        sq_mine = row_sum(mine * mine)
        c3.wait()
        theirs = c3_recv[k]
        cu[k, me] = to_rows([sq_mine + row_sum(theirs * theirs)])
        curved = {}
        for o in peers:
            curved[o] = send(
                cu.at[k, me], cu.at[k, me], cu_ss.at[o], cu_rs.at[k, o], {"samp": flip(me, o)}
            )
        for o in near:
            curved[o].wait()
        sums = cu[k, 0]
        for i in range(1, n_samp):
            sums = sums + cu[k, i]
        (image_sq,) = to_columns(sums, 1)
        alpha = norm_next / (image_sq + pen * dsq)
        r[0] = r[0] - alpha * q[...]
        r[1] = r[1] - alpha * c3_recv[k]
        return norm_next, dsq, alpha, beta

    one = jnp.ones_like(pen)
    zero = jnp.zeros_like(pen)
    _, _, alpha, beta = lax.fori_loop(0, ITERS, step, (one, zero, zero, zero))
    for h in range(2):
        r_out[:, pl.ds(pl.multiple_of(flip(core, h) * half, half), half)] = r[h]
    for o in range(n_samp):
        new = ag[ITERS - 1, o].astype(F32) + beta * d[o]
        columns = pl.ds(pl.multiple_of(flip(me, o) * chunk, chunk), chunk)
        x_out[:, columns] = x[o] + alpha * new


def fused(n_samp, states, targets, penalty):
    rows, columns = states.shape
    channels = targets.shape[1]
    chunk, half = columns // n_samp, rows // 2
    n, c = n_samp, channels
    dma = pltpu.SemaphoreType.DMA
    vmem = pltpu.VMEM
    x_t, r_t = pl.pallas_call(
        functools.partial(kernel, n_samp),
        out_shape=(
            jax.ShapeDtypeStruct((channels, columns), F32),
            jax.ShapeDtypeStruct((channels, rows), F32),
        ),
        in_specs=[
            pl.BlockSpec(memory_space=pl.ANY),
            pl.BlockSpec(memory_space=vmem),
            pl.BlockSpec(memory_space=vmem),
        ],
        out_specs=(pl.BlockSpec(memory_space=vmem), pl.BlockSpec(memory_space=vmem)),
        scratch_shapes=[
            vmem((n, rows, chunk), BF16),
            vmem((c, rows), BF16),
            vmem((2, c, half), F32),
            vmem((c, chunk), F32),
            vmem((n, c, chunk), BF16),
            vmem((ITERS, n, c, chunk), BF16),
            vmem((ITERS, n, c, chunk), BF16),
            vmem((n, c, chunk), F32),
            vmem((n, c, chunk), F32),
            vmem((c, rows), F32),
            vmem((c, half), F32),
            vmem((ITERS, n, 8, c), F32),
            vmem((ITERS, n, 8, c), F32),
            vmem((c, half), BF16),
            vmem((ITERS, c, half), BF16),
            vmem((8, c), F32),
            vmem((ITERS, 8, c), F32),
            vmem((c, half), BF16),
            vmem((ITERS, c, half), BF16),
            vmem((8, c), F32),
            vmem((ITERS, 8, c), F32),
            vmem((ITERS, c, half), F32),
            dma((n, 2)),
            dma((n,)), dma((ITERS, n)),
            dma((n,)), dma((ITERS, n)),
            dma((n,)), dma((ITERS, n)),
            dma((n,)), dma((ITERS, n)),
            dma((5,)), dma((ITERS, 5)),
        ],
        compiler_params=pltpu.CompilerParams(
            collective_id=0, has_side_effects=True, vmem_limit_bytes=52 * 1024 * 1024
        ),
        cost_estimate=pl.CostEstimate(
            flops=4 * ITERS * rows * columns * channels,
            bytes_accessed=2 * rows * columns + 8 * channels * (rows + columns),
            transcendentals=0,
        ),
    )(states, targets.T, penalty[:, None])
    return x_t.T, r_t.T


def plain(states, targets, penalty):
    feat_rows = states.shape[1]

    def weight_sum(value):
        return lax.psum(value, "feat")

    def gradient_of(residual, readout):
        residual_b = residual.astype(BF16)
        partial_value = lax.dot_general(
            states, residual_b, (((0,), (0,)), ((), ())), preferred_element_type=F32
        )
        return lax.psum(partial_value, "samp") - penalty * readout

    readout = jnp.zeros((feat_rows, targets.shape[1]), F32)
    residual = targets
    gradient = gradient_of(residual, readout)
    direction = gradient
    norm_now = weight_sum(jnp.sum(gradient * gradient, axis=0))
    for step in range(ITERS):
        image = lax.psum(
            jnp.dot(states, direction.astype(BF16), preferred_element_type=F32), "feat"
        )
        image_sq = jnp.sum(image * image, axis=0)
        direction_sq = jnp.sum(direction * direction, axis=0)
        curvature = lax.psum(image_sq, "samp") + penalty * weight_sum(direction_sq)
        step_size = norm_now / curvature
        readout = readout + step_size * direction
        residual = residual - step_size * image
        if step + 1 < ITERS:
            gradient = gradient_of(residual, readout)
            norm_next = weight_sum(jnp.sum(gradient * gradient, axis=0))
            direction = gradient + norm_next / norm_now * direction
            norm_now = norm_next
    return (readout, residual)


def solution(mesh):
    n_samp, n_feat = mesh.shape["samp"], mesh.shape["feat"]

    def shards(states, targets, penalty):
        rows, columns = states.shape
        fits = (
            n_samp & (n_samp - 1) == 0
            and n_feat == 4
            and columns % (128 * n_samp) == 0
            and rows % 256 == 0
            and targets.shape[1] == 128
        )
        if fits:
            return fused(n_samp, states, targets, penalty)
        return plain(states, targets, penalty)

    in_specs = (P("samp", "feat"), P("samp", None), P())
    out_specs = (P("feat", None), P("samp", None))
    return jax.shard_map(shards, mesh=mesh, in_specs=in_specs, out_specs=out_specs, check_vma=False)
```

```python
import functools
import jax
import jax.numpy as jnp
from jax import lax
from jax.experimental import pallas as pl
from jax.experimental.pallas import tpu as pltpu
from jax.sharding import PartitionSpec as P

ITERS = 3
F32 = jnp.float32
BF16 = jnp.bfloat16


def flip(index, mask):
    out = index
    bit = 1
    while bit <= mask:
        if mask & bit:
            out = out + bit - 2 * bit * ((index // bit) % 2)
        bit *= 2
    return out


def to_rows(columns):
    channels = columns[0].shape[0]
    lane = lax.broadcasted_iota(jnp.int32, (channels, 128), 1)
    block = jnp.zeros((channels, 128), F32)
    for i, column in enumerate(columns):
        block = jnp.where(lane == i, column, block)
    return jnp.transpose(block)[:8]


def to_columns(rows, count):
    channels = rows.shape[1]
    block = jnp.concatenate([rows, jnp.zeros((128 - 8, channels), F32)], axis=0)
    block = jnp.transpose(block)
    return [block[:, i : i + 1] for i in range(count)]


def kernel(
    n_samp, a_hbm, t_ref, pen_ref, x_out, r_out,
    a, vb, r, acc, rs_send, rs_recv, ag, d, x, qa, q, sm, cu,
    c1_send, c1_recv, c1s_send, c1s_recv, x2_send, x2_recv, x2s_send, x2s_recv, c3_recv,
    a_sem, rs_ss, rs_rs, ag_ss, ag_rs, sm_ss, sm_rs, cu_ss, cu_rs, f_ss, f_rs,
):
    chunk = a.shape[2]
    half = a.shape[1] // 2
    me = lax.axis_index("samp")
    feat = lax.axis_index("feat")
    core = feat % 2
    peers = sorted(range(1, n_samp), key=lambda o: (-(o // 4), o))
    near = list(range(1, n_samp))
    far = [o for o in peers if o % 2 == 0]
    line = [o for o in near if o % 2 == 0]
    beside = {"samp": flip(me, 1)}
    other_core = {"feat": flip(feat, 1)}
    other_x = {"feat": flip(feat, 2)}

    def load(o, h):
        rows = pl.ds(pl.multiple_of(flip(core, h) * half, half), half)
        columns = pl.ds(pl.multiple_of(flip(me, o) * chunk, chunk), chunk)
        return pltpu.make_async_copy(
            a_hbm.at[rows, columns], a.at[o, pl.ds(h * half, half)], a_sem.at[o, h]
        )

    for o in [o + 1 for o in far + [0]] + far + [0]:
        for h in range(2):
            load(o, h).start()

    barrier = pltpu.get_barrier_semaphore()
    for o in near:
        pl.semaphore_signal(barrier, inc=1, device_id={"samp": flip(me, o)})
    for partner in (other_core, other_x):
        pl.semaphore_signal(barrier, inc=1, device_id=partner)

    pen = pen_ref[...]
    for h in range(2):
        r[h] = t_ref[:, pl.ds(pl.multiple_of(flip(core, h) * half, half), half)]
    d[...] = jnp.zeros_like(d)
    x[...] = jnp.zeros_like(x)
    q[...] = jnp.zeros_like(q)
    pl.semaphore_wait(barrier, n_samp - 1 + 2)

    def send(src, dst, ss, rs, target):
        copy = pltpu.make_async_remote_copy(
            src_ref=src, dst_ref=dst, send_sem=ss, recv_sem=rs, device_id=target,
        )
        copy.start()
        return copy

    def row_sum(value):
        return jnp.sum(value, axis=1, keepdims=True)

    def advance(o, last, alpha, beta):
        new = ag[last, o].astype(F32) + beta * d[o]
        d[o] = new
        x[o] = x[o] + alpha * new

    def step(k, carry):
        norm, dsq, alpha, beta = carry
        for h in range(2):
            vb[:, h * half : (h + 1) * half] = r[h].astype(BF16)

        def project(o):
            @pl.when(k == 0)
            def _():
                for h in range(2):
                    load(o, h).wait()

            return jnp.dot(vb[...], a[o], preferred_element_type=F32)

        sent, gathered, small = {}, {}, {}

        def scatter(o, value, target):
            rs_send[o] = value.astype(BF16)
            sent[o] = send(rs_send.at[o], rs_recv.at[k, o], rs_ss.at[o], rs_rs.at[k, o], target)

        for o in far + [0]:
            scatter(o + 1, project(o + 1), beside)
        for o in far:
            value = project(o)
            sent[o + 1].wait_recv()
            scatter(o, value + rs_recv[k, o + 1].astype(F32), {"samp": flip(me, o)})
        acc[...] = project(0)

        @pl.when(k > 0)
        def _():
            for o in range(n_samp):
                advance(o, k - 1, alpha, beta)

        for o in [1] + line:
            sent[o].wait_recv()
            acc[...] += rs_recv[k, o].astype(F32)
        g = acc[...] - pen * x[0]
        gb = g.astype(BF16)
        ag[k, 0] = gb

        def gather(src, o, target):
            gathered[o] = send(ag.at[k, src], ag.at[k, o], ag_ss.at[o], ag_rs.at[k, o], target)

        for o in far:
            gather(0, o, {"samp": flip(me, o)})
        gather(0, 1, beside)
        gf = gb.astype(F32)
        sm[k, me] = to_rows([row_sum(g * g), row_sum(gf * gf), row_sum(gf * d[0])])
        for o in peers:
            small[o] = send(
                sm.at[k, me], sm.at[k, me], sm_ss.at[o], sm_rs.at[k, o], {"samp": flip(me, o)}
            )
        for o in near:
            sent[o].wait_send()

        def image_of(o):
            return lax.dot_general(
                ag[k, o], a[o], (((1,), (1,)), ((), ())), preferred_element_type=F32
            )

        qa[...] = image_of(0)
        for o in line + [1] + [o + 1 for o in line]:
            gathered[o].wait_recv()
            if o % 2 == 0:
                gather(o, o + 1, beside)
            qa[...] += image_of(o)

        c1_send[...] = qa[:, half:].astype(BF16)
        c1 = send(c1_send, c1_recv.at[k], f_ss.at[0], f_rs.at[k, 0], other_core)
        for o in near:
            small[o].wait_recv()
        sums = sm[k, 0]
        for i in range(1, n_samp):
            sums = sums + sm[k, i]
        c1s_send[...] = sums
        c1s = send(c1s_send, c1s_recv.at[k], f_ss.at[1], f_rs.at[k, 1], other_core)
        c1.wait()
        x2_send[...] = (qa[:, :half] + c1_recv[k].astype(F32)).astype(BF16)
        x2 = send(x2_send, x2_recv.at[k], f_ss.at[2], f_rs.at[k, 2], other_x)
        c1s.wait()
        sums = sums + c1s_recv[k]
        x2s_send[...] = sums
        x2s = send(x2s_send, x2s_recv.at[k], f_ss.at[3], f_rs.at[k, 3], other_x)
        for o in near:
            gathered[o].wait_send()
            small[o].wait_send()
        x2s.wait()
        sums = sums + x2s_recv[k]
        norm_next, gbsq, gd = to_columns(sums, 3)
        beta = jnp.where(k == 0, 0.0, norm_next / norm)
        dsq = gbsq + 2.0 * beta * gd + beta * beta * dsq
        x2.wait()
        mine = x2_send[...].astype(F32) + x2_recv[k].astype(F32) + beta * q[...]
        q[...] = mine
        c3 = send(q, c3_recv.at[k], f_ss.at[4], f_rs.at[k, 4], other_core)
        sq_mine = row_sum(mine * mine)
        c3.wait()
        theirs = c3_recv[k]
        cu[k, me] = to_rows([sq_mine + row_sum(theirs * theirs)])
        curved = {}
        for o in peers:
            curved[o] = send(
                cu.at[k, me], cu.at[k, me], cu_ss.at[o], cu_rs.at[k, o], {"samp": flip(me, o)}
            )
        for o in near:
            curved[o].wait()
        sums = cu[k, 0]
        for i in range(1, n_samp):
            sums = sums + cu[k, i]
        (image_sq,) = to_columns(sums, 1)
        alpha = norm_next / (image_sq + pen * dsq)
        r[0] = r[0] - alpha * q[...]
        r[1] = r[1] - alpha * c3_recv[k]
        return norm_next, dsq, alpha, beta

    one = jnp.ones_like(pen)
    zero = jnp.zeros_like(pen)
    _, _, alpha, beta = lax.fori_loop(0, ITERS, step, (one, zero, zero, zero))
    for h in range(2):
        r_out[:, pl.ds(pl.multiple_of(flip(core, h) * half, half), half)] = r[h]
    for o in range(n_samp):
        new = ag[ITERS - 1, o].astype(F32) + beta * d[o]
        columns = pl.ds(pl.multiple_of(flip(me, o) * chunk, chunk), chunk)
        x_out[:, columns] = x[o] + alpha * new


def fused(n_samp, states, targets, penalty):
    rows, columns = states.shape
    channels = targets.shape[1]
    chunk, half = columns // n_samp, rows // 2
    n, c = n_samp, channels
    dma = pltpu.SemaphoreType.DMA
    vmem = pltpu.VMEM
    x_t, r_t = pl.pallas_call(
        functools.partial(kernel, n_samp),
        out_shape=(
            jax.ShapeDtypeStruct((channels, columns), F32),
            jax.ShapeDtypeStruct((channels, rows), F32),
        ),
        in_specs=[
            pl.BlockSpec(memory_space=pl.ANY),
            pl.BlockSpec(memory_space=vmem),
            pl.BlockSpec(memory_space=vmem),
        ],
        out_specs=(pl.BlockSpec(memory_space=vmem), pl.BlockSpec(memory_space=vmem)),
        scratch_shapes=[
            vmem((n, rows, chunk), BF16),
            vmem((c, rows), BF16),
            vmem((2, c, half), F32),
            vmem((c, chunk), F32),
            vmem((n, c, chunk), BF16),
            vmem((ITERS, n, c, chunk), BF16),
            vmem((ITERS, n, c, chunk), BF16),
            vmem((n, c, chunk), F32),
            vmem((n, c, chunk), F32),
            vmem((c, rows), F32),
            vmem((c, half), F32),
            vmem((ITERS, n, 8, c), F32),
            vmem((ITERS, n, 8, c), F32),
            vmem((c, half), BF16),
            vmem((ITERS, c, half), BF16),
            vmem((8, c), F32),
            vmem((ITERS, 8, c), F32),
            vmem((c, half), BF16),
            vmem((ITERS, c, half), BF16),
            vmem((8, c), F32),
            vmem((ITERS, 8, c), F32),
            vmem((ITERS, c, half), F32),
            dma((n, 2)),
            dma((n,)), dma((ITERS, n)),
            dma((n,)), dma((ITERS, n)),
            dma((n,)), dma((ITERS, n)),
            dma((n,)), dma((ITERS, n)),
            dma((5,)), dma((ITERS, 5)),
        ],
        compiler_params=pltpu.CompilerParams(
            collective_id=0, has_side_effects=True, vmem_limit_bytes=52 * 1024 * 1024
        ),
        cost_estimate=pl.CostEstimate(
            flops=4 * ITERS * rows * columns * channels,
            bytes_accessed=2 * rows * columns + 8 * channels * (rows + columns),
            transcendentals=0,
        ),
    )(states, targets.T, penalty[:, None])
    return x_t.T, r_t.T


def plain(states, targets, penalty):
    feat_rows = states.shape[1]

    def weight_sum(value):
        return lax.psum(value, "feat")

    def gradient_of(residual, readout):
        residual_b = residual.astype(BF16)
        partial_value = lax.dot_general(
            states, residual_b, (((0,), (0,)), ((), ())), preferred_element_type=F32
        )
        return lax.psum(partial_value, "samp") - penalty * readout

    readout = jnp.zeros((feat_rows, targets.shape[1]), F32)
    residual = targets
    gradient = gradient_of(residual, readout)
    direction = gradient
    norm_now = weight_sum(jnp.sum(gradient * gradient, axis=0))
    for step in range(ITERS):
        image = lax.psum(
            jnp.dot(states, direction.astype(BF16), preferred_element_type=F32), "feat"
        )
        image_sq = jnp.sum(image * image, axis=0)
        direction_sq = jnp.sum(direction * direction, axis=0)
        curvature = lax.psum(image_sq, "samp") + penalty * weight_sum(direction_sq)
        step_size = norm_now / curvature
        readout = readout + step_size * direction
        residual = residual - step_size * image
        if step + 1 < ITERS:
            gradient = gradient_of(residual, readout)
            norm_next = weight_sum(jnp.sum(gradient * gradient, axis=0))
            direction = gradient + norm_next / norm_now * direction
            norm_now = norm_next
    return (readout, residual)


def solution(mesh):
    n_samp, n_feat = mesh.shape["samp"], mesh.shape["feat"]

    def shards(states, targets, penalty):
        rows, columns = states.shape
        fits = (
            n_samp & (n_samp - 1) == 0
            and n_feat == 4
            and columns % (128 * n_samp) == 0
            and rows % 256 == 0
            and targets.shape[1] == 128
        )
        if fits:
            return fused(n_samp, states, targets, penalty)
        return plain(states, targets, penalty)

    in_specs = (P("samp", "feat"), P("samp", None), P())
    out_specs = (P("feat", None), P("samp", None))
    return jax.shard_map(shards, mesh=mesh, in_specs=in_specs, out_specs=out_specs, check_vma=False)
```

```python
import functools
import jax
import jax.numpy as jnp
from jax import lax
from jax.experimental import pallas as pl
from jax.experimental.pallas import tpu as pltpu
from jax.sharding import PartitionSpec as P

ITERS = 3
F32 = jnp.float32
BF16 = jnp.bfloat16


def flip(index, mask):
    out = index
    bit = 1
    while bit <= mask:
        if mask & bit:
            out = out + bit - 2 * bit * ((index // bit) % 2)
        bit *= 2
    return out


def to_rows(columns):
    channels = columns[0].shape[0]
    lane = lax.broadcasted_iota(jnp.int32, (channels, 128), 1)
    block = jnp.zeros((channels, 128), F32)
    for i, column in enumerate(columns):
        block = jnp.where(lane == i, column, block)
    return jnp.transpose(block)[:8]


def to_columns(rows, count):
    channels = rows.shape[1]
    block = jnp.concatenate([rows, jnp.zeros((128 - 8, channels), F32)], axis=0)
    block = jnp.transpose(block)
    return [block[:, i : i + 1] for i in range(count)]


def kernel(
    n_samp, a_hbm, t_ref, pen_ref, x_out, r_out,
    a, vb, r, acc, rs_send, rs_recv, ag, d, x, qa, q, sm, cu,
    c1_send, c1_recv, c1s_send, c1s_recv, x2_send, x2_recv, x2s_send, x2s_recv, c3_recv,
    a_sem, rs_ss, rs_rs, ag_ss, ag_rs, sm_ss, sm_rs, cu_ss, cu_rs, f_ss, f_rs,
):
    chunk = a.shape[2]
    half = a.shape[1] // 2
    me = lax.axis_index("samp")
    feat = lax.axis_index("feat")
    core = feat % 2
    peers = sorted(range(1, n_samp), key=lambda o: (-(o // 4), o))
    near = list(range(1, n_samp))
    far = [6, 4, 2]
    beside = {"samp": flip(me, 1)}
    other_core = {"feat": flip(feat, 1)}
    other_x = {"feat": flip(feat, 2)}

    def load(o, h):
        rows = pl.ds(pl.multiple_of(flip(core, h) * half, half), half)
        columns = pl.ds(pl.multiple_of(flip(me, o) * chunk, chunk), chunk)
        return pltpu.make_async_copy(
            a_hbm.at[rows, columns], a.at[o, pl.ds(h * half, half)], a_sem.at[o, h]
        )

    for o in [o + 1 for o in far + [0]] + far + [0]:
        for h in range(2):
            load(o, h).start()

    barrier = pltpu.get_barrier_semaphore()
    for o in near:
        pl.semaphore_signal(barrier, inc=1, device_id={"samp": flip(me, o)})
    for partner in (other_core, other_x):
        pl.semaphore_signal(barrier, inc=1, device_id=partner)

    pen = pen_ref[...]
    for h in range(2):
        r[h] = t_ref[:, pl.ds(pl.multiple_of(flip(core, h) * half, half), half)]
    d[...] = jnp.zeros_like(d)
    x[...] = jnp.zeros_like(x)
    q[...] = jnp.zeros_like(q)
    pl.semaphore_wait(barrier, n_samp - 1 + 2)

    def send(src, dst, ss, rs, target):
        copy = pltpu.make_async_remote_copy(
            src_ref=src, dst_ref=dst, send_sem=ss, recv_sem=rs, device_id=target,
        )
        copy.start()
        return copy

    def row_sum(value):
        return jnp.sum(value, axis=1, keepdims=True)

    def advance(o, last, alpha, beta):
        new = ag[last, o].astype(F32) + beta * d[o]
        d[o] = new
        x[o] = x[o] + alpha * new

    def step(k, carry):
        norm, dsq, alpha, beta = carry
        for h in range(2):
            vb[:, h * half : (h + 1) * half] = r[h].astype(BF16)

        def project(o):
            @pl.when(k == 0)
            def _():
                for h in range(2):
                    load(o, h).wait()

            return jnp.dot(vb[...], a[o], preferred_element_type=F32)

        sent, gathered, small = {}, {}, {}

        def scatter(o, value, target):
            rs_send[o] = value.astype(BF16)
            sent[o] = send(rs_send.at[o], rs_recv.at[k, o], rs_ss.at[o], rs_rs.at[k, o], target)

        for o in far + [0]:
            scatter(o + 1, project(o + 1), beside)
        for o in far:
            value = project(o)
            sent[o + 1].wait_recv()
            value = value + rs_recv[k, o + 1].astype(F32)
            if o == 4:
                sent[6].wait_recv()
                value = value + rs_recv[k, 6].astype(F32)
            scatter(o, value, {"samp": flip(me, 4 if o == 4 else 2)})
        acc[...] = project(0)

        @pl.when(k > 0)
        def _():
            for o in range(n_samp):
                advance(o, k - 1, alpha, beta)

        for o in (1, 2, 4):
            sent[o].wait_recv()
            acc[...] += rs_recv[k, o].astype(F32)
        g = acc[...] - pen * x[0]
        gb = g.astype(BF16)
        ag[k, 0] = gb

        def gather(src, o, target):
            gathered[o] = send(ag.at[k, src], ag.at[k, o], ag_ss.at[o], ag_rs.at[k, o], target)

        for o in (4, 2):
            gather(0, o, {"samp": flip(me, o)})
        gather(0, 1, beside)
        gf = gb.astype(F32)
        sm[k, me] = to_rows([row_sum(g * g), row_sum(gf * gf), row_sum(gf * d[0])])
        for o in peers:
            small[o] = send(
                sm.at[k, me], sm.at[k, me], sm_ss.at[o], sm_rs.at[k, o], {"samp": flip(me, o)}
            )
        for o in near:
            sent[o].wait_send()

        def image_of(o):
            return lax.dot_general(
                ag[k, o], a[o], (((1,), (1,)), ((), ())), preferred_element_type=F32
            )

        qa[...] = image_of(0)
        for o in (2, 4, 1, 3, 6, 5, 7):
            gathered[o].wait_recv()
            if o == 4:
                gather(4, 6, {"samp": flip(me, 2)})
            if o % 2 == 0:
                gather(o, o + 1, beside)
            qa[...] += image_of(o)

        c1_send[...] = qa[:, half:].astype(BF16)
        c1 = send(c1_send, c1_recv.at[k], f_ss.at[0], f_rs.at[k, 0], other_core)
        for o in near:
            small[o].wait_recv()
        sums = sm[k, 0]
        for i in range(1, n_samp):
            sums = sums + sm[k, i]
        c1s_send[...] = sums
        c1s = send(c1s_send, c1s_recv.at[k], f_ss.at[1], f_rs.at[k, 1], other_core)
        c1.wait()
        x2_send[...] = (qa[:, :half] + c1_recv[k].astype(F32)).astype(BF16)
        x2 = send(x2_send, x2_recv.at[k], f_ss.at[2], f_rs.at[k, 2], other_x)
        c1s.wait()
        sums = sums + c1s_recv[k]
        x2s_send[...] = sums
        x2s = send(x2s_send, x2s_recv.at[k], f_ss.at[3], f_rs.at[k, 3], other_x)
        for o in near:
            gathered[o].wait_send()
            small[o].wait_send()
        x2s.wait()
        sums = sums + x2s_recv[k]
        norm_next, gbsq, gd = to_columns(sums, 3)
        beta = jnp.where(k == 0, 0.0, norm_next / norm)
        dsq = gbsq + 2.0 * beta * gd + beta * beta * dsq
        x2.wait()
        mine = x2_send[...].astype(F32) + x2_recv[k].astype(F32) + beta * q[...]
        q[...] = mine
        c3 = send(q, c3_recv.at[k], f_ss.at[4], f_rs.at[k, 4], other_core)
        sq_mine = row_sum(mine * mine)
        c3.wait()
        theirs = c3_recv[k]
        cu[k, me] = to_rows([sq_mine + row_sum(theirs * theirs)])
        curved = {}
        for o in peers:
            curved[o] = send(
                cu.at[k, me], cu.at[k, me], cu_ss.at[o], cu_rs.at[k, o], {"samp": flip(me, o)}
            )
        for o in near:
            curved[o].wait()
        sums = cu[k, 0]
        for i in range(1, n_samp):
            sums = sums + cu[k, i]
        (image_sq,) = to_columns(sums, 1)
        alpha = norm_next / (image_sq + pen * dsq)
        r[0] = r[0] - alpha * q[...]
        r[1] = r[1] - alpha * c3_recv[k]
        return norm_next, dsq, alpha, beta

    one = jnp.ones_like(pen)
    zero = jnp.zeros_like(pen)
    _, _, alpha, beta = lax.fori_loop(0, ITERS, step, (one, zero, zero, zero))
    for h in range(2):
        r_out[:, pl.ds(pl.multiple_of(flip(core, h) * half, half), half)] = r[h]
    for o in range(n_samp):
        new = ag[ITERS - 1, o].astype(F32) + beta * d[o]
        columns = pl.ds(pl.multiple_of(flip(me, o) * chunk, chunk), chunk)
        x_out[:, columns] = x[o] + alpha * new


def fused(n_samp, states, targets, penalty):
    rows, columns = states.shape
    channels = targets.shape[1]
    chunk, half = columns // n_samp, rows // 2
    n, c = n_samp, channels
    dma = pltpu.SemaphoreType.DMA
    vmem = pltpu.VMEM
    x_t, r_t = pl.pallas_call(
        functools.partial(kernel, n_samp),
        out_shape=(
            jax.ShapeDtypeStruct((channels, columns), F32),
            jax.ShapeDtypeStruct((channels, rows), F32),
        ),
        in_specs=[
            pl.BlockSpec(memory_space=pl.ANY),
            pl.BlockSpec(memory_space=vmem),
            pl.BlockSpec(memory_space=vmem),
        ],
        out_specs=(pl.BlockSpec(memory_space=vmem), pl.BlockSpec(memory_space=vmem)),
        scratch_shapes=[
            vmem((n, rows, chunk), BF16),
            vmem((c, rows), BF16),
            vmem((2, c, half), F32),
            vmem((c, chunk), F32),
            vmem((n, c, chunk), BF16),
            vmem((ITERS, n, c, chunk), BF16),
            vmem((ITERS, n, c, chunk), BF16),
            vmem((n, c, chunk), F32),
            vmem((n, c, chunk), F32),
            vmem((c, rows), F32),
            vmem((c, half), F32),
            vmem((ITERS, n, 8, c), F32),
            vmem((ITERS, n, 8, c), F32),
            vmem((c, half), BF16),
            vmem((ITERS, c, half), BF16),
            vmem((8, c), F32),
            vmem((ITERS, 8, c), F32),
            vmem((c, half), BF16),
            vmem((ITERS, c, half), BF16),
            vmem((8, c), F32),
            vmem((ITERS, 8, c), F32),
            vmem((ITERS, c, half), F32),
            dma((n, 2)),
            dma((n,)), dma((ITERS, n)),
            dma((n,)), dma((ITERS, n)),
            dma((n,)), dma((ITERS, n)),
            dma((n,)), dma((ITERS, n)),
            dma((5,)), dma((ITERS, 5)),
        ],
        compiler_params=pltpu.CompilerParams(
            collective_id=0, has_side_effects=True, vmem_limit_bytes=52 * 1024 * 1024
        ),
        cost_estimate=pl.CostEstimate(
            flops=4 * ITERS * rows * columns * channels,
            bytes_accessed=2 * rows * columns + 8 * channels * (rows + columns),
            transcendentals=0,
        ),
    )(states, targets.T, penalty[:, None])
    return x_t.T, r_t.T


def plain(states, targets, penalty):
    feat_rows = states.shape[1]

    def weight_sum(value):
        return lax.psum(value, "feat")

    def gradient_of(residual, readout):
        residual_b = residual.astype(BF16)
        partial_value = lax.dot_general(
            states, residual_b, (((0,), (0,)), ((), ())), preferred_element_type=F32
        )
        return lax.psum(partial_value, "samp") - penalty * readout

    readout = jnp.zeros((feat_rows, targets.shape[1]), F32)
    residual = targets
    gradient = gradient_of(residual, readout)
    direction = gradient
    norm_now = weight_sum(jnp.sum(gradient * gradient, axis=0))
    for step in range(ITERS):
        image = lax.psum(
            jnp.dot(states, direction.astype(BF16), preferred_element_type=F32), "feat"
        )
        image_sq = jnp.sum(image * image, axis=0)
        direction_sq = jnp.sum(direction * direction, axis=0)
        curvature = lax.psum(image_sq, "samp") + penalty * weight_sum(direction_sq)
        step_size = norm_now / curvature
        readout = readout + step_size * direction
        residual = residual - step_size * image
        if step + 1 < ITERS:
            gradient = gradient_of(residual, readout)
            norm_next = weight_sum(jnp.sum(gradient * gradient, axis=0))
            direction = gradient + norm_next / norm_now * direction
            norm_now = norm_next
    return (readout, residual)


def solution(mesh):
    n_samp, n_feat = mesh.shape["samp"], mesh.shape["feat"]

    def shards(states, targets, penalty):
        rows, columns = states.shape
        fits = (
            n_samp == 8
            and n_feat == 4
            and columns % (128 * n_samp) == 0
            and rows % 256 == 0
            and targets.shape[1] == 128
        )
        if fits:
            return fused(n_samp, states, targets, penalty)
        return plain(states, targets, penalty)

    in_specs = (P("samp", "feat"), P("samp", None), P())
    out_specs = (P("feat", None), P("samp", None))
    return jax.shard_map(shards, mesh=mesh, in_specs=in_specs, out_specs=out_specs, check_vma=False)
```

```python
import functools
import jax
import jax.numpy as jnp
from jax import lax
from jax.experimental import pallas as pl
from jax.experimental.pallas import tpu as pltpu
from jax.sharding import PartitionSpec as P

ITERS = 3
F32 = jnp.float32
BF16 = jnp.bfloat16


def flip(index, mask):
    out = index
    bit = 1
    while bit <= mask:
        if mask & bit:
            out = out + bit - 2 * bit * ((index // bit) % 2)
        bit *= 2
    return out


def to_rows(columns):
    channels = columns[0].shape[0]
    lane = lax.broadcasted_iota(jnp.int32, (channels, 128), 1)
    block = jnp.zeros((channels, 128), F32)
    for i, column in enumerate(columns):
        block = jnp.where(lane == i, column, block)
    return jnp.transpose(block)[:8]


def to_columns(rows, count):
    channels = rows.shape[1]
    block = jnp.concatenate([rows, jnp.zeros((128 - 8, channels), F32)], axis=0)
    block = jnp.transpose(block)
    return [block[:, i : i + 1] for i in range(count)]


def kernel(
    n_samp, a_hbm, t_ref, pen_ref, x_out, r_out,
    a, vb, r, acc, rs_send, rs_recv, ag, d, x, qa, q, sm, cu,
    c1_send, c1_recv, c1s_send, c1s_recv, x2_send, x2_recv, x2s_send, x2s_recv, c3_recv,
    a_sem, rs_ss, rs_rs, ag_ss, ag_rs, sm_ss, sm_rs, cu_ss, cu_rs, f_ss, f_rs,
):
    chunk = a.shape[2]
    half = a.shape[1] // 2
    me = lax.axis_index("samp")
    feat = lax.axis_index("feat")
    core = feat % 2
    peers = sorted(range(1, n_samp), key=lambda o: (-(o // 4), o))
    near = list(range(1, n_samp))
    far = [o for o in peers if o % 2 == 0]
    line = [o for o in near if o % 2 == 0]
    beside = {"samp": flip(me, 1)}
    other_core = {"feat": flip(feat, 1)}
    other_x = {"feat": flip(feat, 2)}

    def load(o, h):
        rows = pl.ds(pl.multiple_of(flip(core, h) * half, half), half)
        columns = pl.ds(pl.multiple_of(flip(me, o) * chunk, chunk), chunk)
        return pltpu.make_async_copy(
            a_hbm.at[rows, columns], a.at[o, pl.ds(h * half, half)], a_sem.at[o, h]
        )

    for o in [o + 1 for o in far + [0]] + far + [0]:
        for h in range(2):
            load(o, h).start()

    barrier = pltpu.get_barrier_semaphore()
    for o in near:
        pl.semaphore_signal(barrier, inc=1, device_id={"samp": flip(me, o)})
    for partner in (other_core, other_x):
        pl.semaphore_signal(barrier, inc=1, device_id=partner)

    pen = pen_ref[...]
    for h in range(2):
        r[h] = t_ref[:, pl.ds(pl.multiple_of(flip(core, h) * half, half), half)]
    d[...] = jnp.zeros_like(d)
    x[...] = jnp.zeros_like(x)
    q[...] = jnp.zeros_like(q)
    pl.semaphore_wait(barrier, n_samp - 1 + 2)

    def send(src, dst, ss, rs, target):
        copy = pltpu.make_async_remote_copy(
            src_ref=src, dst_ref=dst, send_sem=ss, recv_sem=rs, device_id=target,
        )
        copy.start()
        return copy

    def row_sum(value):
        return jnp.sum(value, axis=1, keepdims=True)

    def advance(o, last, alpha, beta):
        new = ag[last, o].astype(F32) + beta * d[o]
        d[o] = new
        x[o] = x[o] + alpha * new

    def step(k, carry):
        norm, dsq, alpha, beta = carry
        for h in range(2):
            vb[:, h * half : (h + 1) * half] = r[h].astype(BF16)

        def project(o):
            @pl.when(k == 0)
            def _():
                for h in range(2):
                    load(o, h).wait()

            return jnp.dot(vb[...], a[o], preferred_element_type=F32)

        sent, gathered, small = {}, {}, {}

        def scatter(o, value, target):
            rs_send[o] = value.astype(BF16)
            sent[o] = send(rs_send.at[o], rs_recv.at[k, o], rs_ss.at[o], rs_rs.at[k, o], target)

        for o in far + [0]:
            scatter(o + 1, project(o + 1), beside)
        for o in far:
            value = project(o)
            sent[o + 1].wait_recv()
            scatter(o, value + rs_recv[k, o + 1].astype(F32), {"samp": flip(me, o)})
        acc[...] = project(0)

        @pl.when(k > 0)
        def _():
            for o in range(n_samp):
                advance(o, k - 1, alpha, beta)

        for o in [1] + line:
            sent[o].wait_recv()
            acc[...] += rs_recv[k, o].astype(F32)
        g = acc[...] - pen * x[0]
        gb = g.astype(BF16)
        ag[k, 0] = gb

        def gather(src, o, target):
            gathered[o] = send(ag.at[k, src], ag.at[k, o], ag_ss.at[o], ag_rs.at[k, o], target)

        gather(0, 1, beside)
        for o in line:
            gather(0, o, {"samp": flip(me, o)})
        gf = gb.astype(F32)
        sm[k, me] = to_rows([row_sum(g * g), row_sum(gf * gf), row_sum(gf * d[0])])
        for o in peers:
            small[o] = send(
                sm.at[k, me], sm.at[k, me], sm_ss.at[o], sm_rs.at[k, o], {"samp": flip(me, o)}
            )
        for o in near:
            sent[o].wait_send()

        def image_of(o):
            return lax.dot_general(
                ag[k, o], a[o], (((1,), (1,)), ((), ())), preferred_element_type=F32
            )

        qa[...] = image_of(0)
        for o in line:
            gathered[o].wait_recv()
            gather(o, o + 1, beside)
        for o in line + [1] + [o + 1 for o in line]:
            if o % 2 == 1:
                gathered[o].wait_recv()
            qa[...] += image_of(o)

        c1_send[...] = qa[:, half:].astype(BF16)
        c1 = send(c1_send, c1_recv.at[k], f_ss.at[0], f_rs.at[k, 0], other_core)
        for o in near:
            small[o].wait_recv()
        sums = sm[k, 0]
        for i in range(1, n_samp):
            sums = sums + sm[k, i]
        c1s_send[...] = sums
        c1s = send(c1s_send, c1s_recv.at[k], f_ss.at[1], f_rs.at[k, 1], other_core)
        c1.wait()
        x2_send[...] = (qa[:, :half] + c1_recv[k].astype(F32)).astype(BF16)
        x2 = send(x2_send, x2_recv.at[k], f_ss.at[2], f_rs.at[k, 2], other_x)
        c1s.wait()
        sums = sums + c1s_recv[k]
        x2s_send[...] = sums
        x2s = send(x2s_send, x2s_recv.at[k], f_ss.at[3], f_rs.at[k, 3], other_x)
        for o in near:
            gathered[o].wait_send()
            small[o].wait_send()
        x2s.wait()
        sums = sums + x2s_recv[k]
        norm_next, gbsq, gd = to_columns(sums, 3)
        beta = jnp.where(k == 0, 0.0, norm_next / norm)
        dsq = gbsq + 2.0 * beta * gd + beta * beta * dsq
        x2.wait()
        mine = x2_send[...].astype(F32) + x2_recv[k].astype(F32) + beta * q[...]
        q[...] = mine
        c3 = send(q, c3_recv.at[k], f_ss.at[4], f_rs.at[k, 4], other_core)
        sq_mine = row_sum(mine * mine)
        c3.wait()
        theirs = c3_recv[k]
        cu[k, me] = to_rows([sq_mine + row_sum(theirs * theirs)])
        curved = {}
        for o in peers:
            curved[o] = send(
                cu.at[k, me], cu.at[k, me], cu_ss.at[o], cu_rs.at[k, o], {"samp": flip(me, o)}
            )
        for o in near:
            curved[o].wait()
        sums = cu[k, 0]
        for i in range(1, n_samp):
            sums = sums + cu[k, i]
        (image_sq,) = to_columns(sums, 1)
        alpha = norm_next / (image_sq + pen * dsq)
        r[0] = r[0] - alpha * q[...]
        r[1] = r[1] - alpha * c3_recv[k]
        return norm_next, dsq, alpha, beta

    one = jnp.ones_like(pen)
    zero = jnp.zeros_like(pen)
    _, _, alpha, beta = lax.fori_loop(0, ITERS, step, (one, zero, zero, zero))
    for h in range(2):
        r_out[:, pl.ds(pl.multiple_of(flip(core, h) * half, half), half)] = r[h]
    for o in range(n_samp):
        new = ag[ITERS - 1, o].astype(F32) + beta * d[o]
        columns = pl.ds(pl.multiple_of(flip(me, o) * chunk, chunk), chunk)
        x_out[:, columns] = x[o] + alpha * new


def fused(n_samp, states, targets, penalty):
    rows, columns = states.shape
    channels = targets.shape[1]
    chunk, half = columns // n_samp, rows // 2
    n, c = n_samp, channels
    dma = pltpu.SemaphoreType.DMA
    vmem = pltpu.VMEM
    x_t, r_t = pl.pallas_call(
        functools.partial(kernel, n_samp),
        out_shape=(
            jax.ShapeDtypeStruct((channels, columns), F32),
            jax.ShapeDtypeStruct((channels, rows), F32),
        ),
        in_specs=[
            pl.BlockSpec(memory_space=pl.ANY),
            pl.BlockSpec(memory_space=vmem),
            pl.BlockSpec(memory_space=vmem),
        ],
        out_specs=(pl.BlockSpec(memory_space=vmem), pl.BlockSpec(memory_space=vmem)),
        scratch_shapes=[
            vmem((n, rows, chunk), BF16),
            vmem((c, rows), BF16),
            vmem((2, c, half), F32),
            vmem((c, chunk), F32),
            vmem((n, c, chunk), BF16),
            vmem((ITERS, n, c, chunk), BF16),
            vmem((ITERS, n, c, chunk), BF16),
            vmem((n, c, chunk), F32),
            vmem((n, c, chunk), F32),
            vmem((c, rows), F32),
            vmem((c, half), F32),
            vmem((ITERS, n, 8, c), F32),
            vmem((ITERS, n, 8, c), F32),
            vmem((c, half), BF16),
            vmem((ITERS, c, half), BF16),
            vmem((8, c), F32),
            vmem((ITERS, 8, c), F32),
            vmem((c, half), BF16),
            vmem((ITERS, c, half), BF16),
            vmem((8, c), F32),
            vmem((ITERS, 8, c), F32),
            vmem((ITERS, c, half), F32),
            dma((n, 2)),
            dma((n,)), dma((ITERS, n)),
            dma((n,)), dma((ITERS, n)),
            dma((n,)), dma((ITERS, n)),
            dma((n,)), dma((ITERS, n)),
            dma((5,)), dma((ITERS, 5)),
        ],
        compiler_params=pltpu.CompilerParams(
            collective_id=0, has_side_effects=True, vmem_limit_bytes=52 * 1024 * 1024
        ),
        cost_estimate=pl.CostEstimate(
            flops=4 * ITERS * rows * columns * channels,
            bytes_accessed=2 * rows * columns + 8 * channels * (rows + columns),
            transcendentals=0,
        ),
    )(states, targets.T, penalty[:, None])
    return x_t.T, r_t.T


def plain(states, targets, penalty):
    feat_rows = states.shape[1]

    def weight_sum(value):
        return lax.psum(value, "feat")

    def gradient_of(residual, readout):
        residual_b = residual.astype(BF16)
        partial_value = lax.dot_general(
            states, residual_b, (((0,), (0,)), ((), ())), preferred_element_type=F32
        )
        return lax.psum(partial_value, "samp") - penalty * readout

    readout = jnp.zeros((feat_rows, targets.shape[1]), F32)
    residual = targets
    gradient = gradient_of(residual, readout)
    direction = gradient
    norm_now = weight_sum(jnp.sum(gradient * gradient, axis=0))
    for step in range(ITERS):
        image = lax.psum(
            jnp.dot(states, direction.astype(BF16), preferred_element_type=F32), "feat"
        )
        image_sq = jnp.sum(image * image, axis=0)
        direction_sq = jnp.sum(direction * direction, axis=0)
        curvature = lax.psum(image_sq, "samp") + penalty * weight_sum(direction_sq)
        step_size = norm_now / curvature
        readout = readout + step_size * direction
        residual = residual - step_size * image
        if step + 1 < ITERS:
            gradient = gradient_of(residual, readout)
            norm_next = weight_sum(jnp.sum(gradient * gradient, axis=0))
            direction = gradient + norm_next / norm_now * direction
            norm_now = norm_next
    return (readout, residual)


def solution(mesh):
    n_samp, n_feat = mesh.shape["samp"], mesh.shape["feat"]

    def shards(states, targets, penalty):
        rows, columns = states.shape
        fits = (
            n_samp & (n_samp - 1) == 0
            and n_feat == 4
            and columns % (128 * n_samp) == 0
            and rows % 256 == 0
            and targets.shape[1] == 128
        )
        if fits:
            return fused(n_samp, states, targets, penalty)
        return plain(states, targets, penalty)

    in_specs = (P("samp", "feat"), P("samp", None), P())
    out_specs = (P("feat", None), P("samp", None))
    return jax.shard_map(shards, mesh=mesh, in_specs=in_specs, out_specs=out_specs, check_vma=False)
```

```python
import functools
import jax
import jax.numpy as jnp
from jax import lax
from jax.experimental import pallas as pl
from jax.experimental.pallas import tpu as pltpu
from jax.sharding import PartitionSpec as P

ITERS = 3
F32 = jnp.float32
BF16 = jnp.bfloat16


def flip(index, mask):
    out = index
    bit = 1
    while bit <= mask:
        if mask & bit:
            out = out + bit - 2 * bit * ((index // bit) % 2)
        bit *= 2
    return out


def to_rows(columns):
    channels = columns[0].shape[0]
    lane = lax.broadcasted_iota(jnp.int32, (channels, 128), 1)
    block = jnp.zeros((channels, 128), F32)
    for i, column in enumerate(columns):
        block = jnp.where(lane == i, column, block)
    return jnp.transpose(block)[:8]


def to_columns(rows, count):
    channels = rows.shape[1]
    block = jnp.concatenate([rows, jnp.zeros((128 - 8, channels), F32)], axis=0)
    block = jnp.transpose(block)
    return [block[:, i : i + 1] for i in range(count)]


def kernel(
    n_samp, a_hbm, t_ref, pen_ref, x_out, r_out,
    a, vb, r, acc, rs_send, rs_recv, ag, d, x, qa, q, sm, cu,
    c1_send, c1_recv, c1s_send, c1s_recv, x2_send, x2_recv, x2s_send, x2s_recv, c3_recv,
    a_sem, rs_ss, rs_rs, ag_ss, ag_rs, sm_ss, sm_rs, cu_ss, cu_rs, f_ss, f_rs,
):
    chunk = a.shape[2]
    half = a.shape[1] // 2
    me = lax.axis_index("samp")
    feat = lax.axis_index("feat")
    core = feat % 2
    peers = sorted(range(1, n_samp), key=lambda o: (-(o // 4), o))
    near = list(range(1, n_samp))
    far = [o for o in peers if o % 2 == 0]
    line = [o for o in near if o % 2 == 0]
    beside = {"samp": flip(me, 1)}
    along = {"samp": flip(me, 2)}
    other_core = {"feat": flip(feat, 1)}
    other_x = {"feat": flip(feat, 2)}

    def load(o, h):
        rows = pl.ds(pl.multiple_of(flip(core, h) * half, half), half)
        columns = pl.ds(pl.multiple_of(flip(me, o) * chunk, chunk), chunk)
        return pltpu.make_async_copy(
            a_hbm.at[rows, columns], a.at[o, pl.ds(h * half, half)], a_sem.at[o, h]
        )

    for o in [o + 1 for o in far + [0]] + far + [0]:
        for h in range(2):
            load(o, h).start()

    barrier = pltpu.get_barrier_semaphore()
    for o in near:
        pl.semaphore_signal(barrier, inc=1, device_id={"samp": flip(me, o)})
    for partner in (other_core, other_x):
        pl.semaphore_signal(barrier, inc=1, device_id=partner)

    pen = pen_ref[...]
    for h in range(2):
        r[h] = t_ref[:, pl.ds(pl.multiple_of(flip(core, h) * half, half), half)]
    d[...] = jnp.zeros_like(d)
    x[...] = jnp.zeros_like(x)
    q[...] = jnp.zeros_like(q)
    pl.semaphore_wait(barrier, n_samp - 1 + 2)

    def send(src, dst, ss, rs, target):
        copy = pltpu.make_async_remote_copy(
            src_ref=src, dst_ref=dst, send_sem=ss, recv_sem=rs, device_id=target,
        )
        copy.start()
        return copy

    def row_sum(value):
        return jnp.sum(value, axis=1, keepdims=True)

    def advance(o, last, alpha, beta):
        new = ag[last, o].astype(F32) + beta * d[o]
        d[o] = new
        x[o] = x[o] + alpha * new

    def step(k, carry):
        norm, dsq, alpha, beta = carry
        for h in range(2):
            vb[:, h * half : (h + 1) * half] = r[h].astype(BF16)

        def project(o):
            @pl.when(k == 0)
            def _():
                for h in range(2):
                    load(o, h).wait()

            return jnp.dot(vb[...], a[o], preferred_element_type=F32)

        sent, gathered, small = {}, {}, {}

        def scatter(o, value, target):
            rs_send[o] = value.astype(BF16)
            sent[o] = send(rs_send.at[o], rs_recv.at[k, o], rs_ss.at[o], rs_rs.at[k, o], target)

        for o in (4, 6):
            scatter(o + 1, project(o + 1), beside)
        scatter(3, project(3), along)
        for o in (4, 6):
            value = project(o)
            sent[o + 1].wait_recv()
            scatter(o, value + rs_recv[k, o + 1].astype(F32), {"samp": flip(me, o)})
        value = project(1)
        sent[3].wait_recv()
        scatter(1, value + rs_recv[k, 3].astype(F32), beside)
        scatter(2, project(2), along)
        acc[...] = project(0)

        @pl.when(k > 0)
        def _():
            for o in range(n_samp):
                advance(o, k - 1, alpha, beta)

        for o in [1] + line:
            sent[o].wait_recv()
            acc[...] += rs_recv[k, o].astype(F32)
        g = acc[...] - pen * x[0]
        gb = g.astype(BF16)
        ag[k, 0] = gb

        def gather(src, o, target):
            gathered[o] = send(ag.at[k, src], ag.at[k, o], ag_ss.at[o], ag_rs.at[k, o], target)

        gather(0, 1, beside)
        for o in line:
            gather(0, o, {"samp": flip(me, o)})
        gf = gb.astype(F32)
        sm[k, me] = to_rows([row_sum(g * g), row_sum(gf * gf), row_sum(gf * d[0])])
        for o in peers:
            small[o] = send(
                sm.at[k, me], sm.at[k, me], sm_ss.at[o], sm_rs.at[k, o], {"samp": flip(me, o)}
            )
        for o in near:
            sent[o].wait_send()

        def image_of(o):
            return lax.dot_general(
                ag[k, o], a[o], (((1,), (1,)), ((), ())), preferred_element_type=F32
            )

        qa[...] = image_of(0)
        gathered[1].wait_recv()
        gather(1, 3, along)
        for o in line:
            gathered[o].wait_recv()
            if o > 2:
                gather(o, o + 1, beside)
        for o in line + [1] + [o + 1 for o in line]:
            if o in (3, 5, 7):
                gathered[o].wait_recv()
            qa[...] += image_of(o)

        c1_send[...] = qa[:, half:].astype(BF16)
        c1 = send(c1_send, c1_recv.at[k], f_ss.at[0], f_rs.at[k, 0], other_core)
        for o in near:
            small[o].wait_recv()
        sums = sm[k, 0]
        for i in range(1, n_samp):
            sums = sums + sm[k, i]
        c1s_send[...] = sums
        c1s = send(c1s_send, c1s_recv.at[k], f_ss.at[1], f_rs.at[k, 1], other_core)
        c1.wait()
        x2_send[...] = (qa[:, :half] + c1_recv[k].astype(F32)).astype(BF16)
        x2 = send(x2_send, x2_recv.at[k], f_ss.at[2], f_rs.at[k, 2], other_x)
        c1s.wait()
        sums = sums + c1s_recv[k]
        x2s_send[...] = sums
        x2s = send(x2s_send, x2s_recv.at[k], f_ss.at[3], f_rs.at[k, 3], other_x)
        for o in near:
            gathered[o].wait_send()
            small[o].wait_send()
        x2s.wait()
        sums = sums + x2s_recv[k]
        norm_next, gbsq, gd = to_columns(sums, 3)
        beta = jnp.where(k == 0, 0.0, norm_next / norm)
        dsq = gbsq + 2.0 * beta * gd + beta * beta * dsq
        x2.wait()
        mine = x2_send[...].astype(F32) + x2_recv[k].astype(F32) + beta * q[...]
        q[...] = mine
        c3 = send(q, c3_recv.at[k], f_ss.at[4], f_rs.at[k, 4], other_core)
        sq_mine = row_sum(mine * mine)
        c3.wait()
        theirs = c3_recv[k]
        cu[k, me] = to_rows([sq_mine + row_sum(theirs * theirs)])
        curved = {}
        for o in peers:
            curved[o] = send(
                cu.at[k, me], cu.at[k, me], cu_ss.at[o], cu_rs.at[k, o], {"samp": flip(me, o)}
            )
        for o in near:
            curved[o].wait()
        sums = cu[k, 0]
        for i in range(1, n_samp):
            sums = sums + cu[k, i]
        (image_sq,) = to_columns(sums, 1)
        alpha = norm_next / (image_sq + pen * dsq)
        r[0] = r[0] - alpha * q[...]
        r[1] = r[1] - alpha * c3_recv[k]
        return norm_next, dsq, alpha, beta

    one = jnp.ones_like(pen)
    zero = jnp.zeros_like(pen)
    _, _, alpha, beta = lax.fori_loop(0, ITERS, step, (one, zero, zero, zero))
    for h in range(2):
        r_out[:, pl.ds(pl.multiple_of(flip(core, h) * half, half), half)] = r[h]
    for o in range(n_samp):
        new = ag[ITERS - 1, o].astype(F32) + beta * d[o]
        columns = pl.ds(pl.multiple_of(flip(me, o) * chunk, chunk), chunk)
        x_out[:, columns] = x[o] + alpha * new


def fused(n_samp, states, targets, penalty):
    rows, columns = states.shape
    channels = targets.shape[1]
    chunk, half = columns // n_samp, rows // 2
    n, c = n_samp, channels
    dma = pltpu.SemaphoreType.DMA
    vmem = pltpu.VMEM
    x_t, r_t = pl.pallas_call(
        functools.partial(kernel, n_samp),
        out_shape=(
            jax.ShapeDtypeStruct((channels, columns), F32),
            jax.ShapeDtypeStruct((channels, rows), F32),
        ),
        in_specs=[
            pl.BlockSpec(memory_space=pl.ANY),
            pl.BlockSpec(memory_space=vmem),
            pl.BlockSpec(memory_space=vmem),
        ],
        out_specs=(pl.BlockSpec(memory_space=vmem), pl.BlockSpec(memory_space=vmem)),
        scratch_shapes=[
            vmem((n, rows, chunk), BF16),
            vmem((c, rows), BF16),
            vmem((2, c, half), F32),
            vmem((c, chunk), F32),
            vmem((n, c, chunk), BF16),
            vmem((ITERS, n, c, chunk), BF16),
            vmem((ITERS, n, c, chunk), BF16),
            vmem((n, c, chunk), F32),
            vmem((n, c, chunk), F32),
            vmem((c, rows), F32),
            vmem((c, half), F32),
            vmem((ITERS, n, 8, c), F32),
            vmem((ITERS, n, 8, c), F32),
            vmem((c, half), BF16),
            vmem((ITERS, c, half), BF16),
            vmem((8, c), F32),
            vmem((ITERS, 8, c), F32),
            vmem((c, half), BF16),
            vmem((ITERS, c, half), BF16),
            vmem((8, c), F32),
            vmem((ITERS, 8, c), F32),
            vmem((ITERS, c, half), F32),
            dma((n, 2)),
            dma((n,)), dma((ITERS, n)),
            dma((n,)), dma((ITERS, n)),
            dma((n,)), dma((ITERS, n)),
            dma((n,)), dma((ITERS, n)),
            dma((5,)), dma((ITERS, 5)),
        ],
        compiler_params=pltpu.CompilerParams(
            collective_id=0, has_side_effects=True, vmem_limit_bytes=52 * 1024 * 1024
        ),
        cost_estimate=pl.CostEstimate(
            flops=4 * ITERS * rows * columns * channels,
            bytes_accessed=2 * rows * columns + 8 * channels * (rows + columns),
            transcendentals=0,
        ),
    )(states, targets.T, penalty[:, None])
    return x_t.T, r_t.T


def plain(states, targets, penalty):
    feat_rows = states.shape[1]

    def weight_sum(value):
        return lax.psum(value, "feat")

    def gradient_of(residual, readout):
        residual_b = residual.astype(BF16)
        partial_value = lax.dot_general(
            states, residual_b, (((0,), (0,)), ((), ())), preferred_element_type=F32
        )
        return lax.psum(partial_value, "samp") - penalty * readout

    readout = jnp.zeros((feat_rows, targets.shape[1]), F32)
    residual = targets
    gradient = gradient_of(residual, readout)
    direction = gradient
    norm_now = weight_sum(jnp.sum(gradient * gradient, axis=0))
    for step in range(ITERS):
        image = lax.psum(
            jnp.dot(states, direction.astype(BF16), preferred_element_type=F32), "feat"
        )
        image_sq = jnp.sum(image * image, axis=0)
        direction_sq = jnp.sum(direction * direction, axis=0)
        curvature = lax.psum(image_sq, "samp") + penalty * weight_sum(direction_sq)
        step_size = norm_now / curvature
        readout = readout + step_size * direction
        residual = residual - step_size * image
        if step + 1 < ITERS:
            gradient = gradient_of(residual, readout)
            norm_next = weight_sum(jnp.sum(gradient * gradient, axis=0))
            direction = gradient + norm_next / norm_now * direction
            norm_now = norm_next
    return (readout, residual)


def solution(mesh):
    n_samp, n_feat = mesh.shape["samp"], mesh.shape["feat"]

    def shards(states, targets, penalty):
        rows, columns = states.shape
        fits = (
            n_samp == 8
            and n_feat == 4
            and columns % (128 * n_samp) == 0
            and rows % 256 == 0
            and targets.shape[1] == 128
        )
        if fits:
            return fused(n_samp, states, targets, penalty)
        return plain(states, targets, penalty)

    in_specs = (P("samp", "feat"), P("samp", None), P())
    out_specs = (P("feat", None), P("samp", None))
    return jax.shard_map(shards, mesh=mesh, in_specs=in_specs, out_specs=out_specs, check_vma=False)
```
